32 devices in a mesh: dp: 2 (over x), expert: 16 (over z, y, core).
Axes of the slice: x: 2, y: 2, z: 4, core: 2. Of those that a mesh axis runs over, the one named last changes fastest.
Arguments:
- tokens: bfloat16 [1792, 2048], P(('dp', 'expert')), may hold values from -6 to 6
- expert_ids: int32 [1792, 8], P(('dp', 'expert')), may hold values from 0 to 15, all different within a row; in each aligned block of 56 rows (0 to 55, 56 to 111, ...) at most 32 rows name the same one
- combine: float32 [1792, 8], P(('dp', 'expert')), may hold values from 0.2 to 1
- w_gate: bfloat16 [16, 2048, 768], P('expert'), may hold values from -0.125 to 0.125
- w_up: bfloat16 [16, 2048, 768], P('expert'), may hold values from -0.125 to 0.125
- w_down: bfloat16 [16, 768, 2048], P('expert'), may hold values from -0.21875 to 0.21875
- grad_out: bfloat16 [1792, 2048], P(('dp', 'expert')), may hold values from -6 to 6
Outputs:
- mixed: bfloat16 [1792, 2048], P(('dp', 'expert'))
- grad_tokens: bfloat16 [1792, 2048], P(('dp', 'expert'))
- grad_gate: bfloat16 [16, 2048, 768], P('expert', 'dp')
- grad_up: bfloat16 [16, 2048, 768], P('expert', 'dp')
- grad_down: bfloat16 [16, 768, 2048], P('expert', None, 'dp')
The draws below stay inside these ranges and needn't reach their ends.
Inputs may be any that keep to these rules, and one draw needn't show every extreme that they name: `expert_ids`: each row names 8 different experts. Within the 56 rows of one device no expert is named by more than 32 rows, and in every draw some expert is named by exactly 32 rows of some device.
All inputs are finite; a program needn't handle non-finite values.
Results may differ from the reference program's by a relative error of at most 0.017.
Values may be sent and summed in bfloat16 or wider, within the bound.
A program may use at most 128 MiB of HBM per device.

```python
import math
import jax
import jax.numpy as jnp
import numpy as np
from jax import lax

D = 2048
H = 768
TOPK = 8
TOK_DEV = 56
EXPERTS = 16
CAP = 32
TOKENS = 1792
N_DP = 2
N_EXPERT = 16


def levels(rng, dims, split, smallest, high):
    factor_of = 1.0
    for position, shards_of in split:
        heights = jax.random.uniform(jax.random.fold_in(jax.random.fold_in(rng, 6), position), (shards_of,), jnp.float32, smallest / len(split), high / len(split))
        factor_of = factor_of * jnp.repeat(jnp.exp(heights), dims[position] // shards_of).reshape((-1,) + (1,) * (len(dims) - 1 - position))
    return factor_of


def shared_out(key, own, number, rows, amount, top, limit, skew):
    sequence = jax.random.permutation(key, amount)
    packed, usual = portions_of(amount, rows * top, limit, skew, True), portions_of(amount, rows * top, limit, skew, False)
    places = jnp.arange(amount)

    def named(lengths, offset_by):
        used = int((lengths > 0).sum())
        fixed = max(1, used // 4)
        shifted = fixed + (places - fixed + offset_by * (used - fixed)) % max(1, amount - fixed)
        return jnp.zeros((amount,), jnp.int32).at[sequence[jnp.where(places < fixed, places, shifted)]].set(jnp.asarray(lengths, jnp.int32))

    lengths = jnp.where(number % 4 == 0, named(packed, number // 4), named(usual, number - number // 4 - 1))
    mixed = jax.random.permutation(jax.random.fold_in(own, 3), amount)
    donor, sink = mixed[0:amount // 2 * 2:2], mixed[1:amount // 2 * 2:2]
    slack = jnp.minimum(lengths[donor] - 1, limit - lengths[sink]) // 2
    slack = jnp.where((donor == sequence[0]) | (sink == sequence[0]) | (lengths[sink] == 0), 0, jnp.maximum(slack, 0))
    shifted = jax.random.randint(jax.random.fold_in(own, 4), (amount // 2,), 0, 1 << 20) % (slack + 1)
    lengths = lengths.at[donor].add(-shifted).at[sink].add(shifted)
    items = jnp.searchsorted(jnp.cumsum(lengths), jnp.arange(rows * top), side="right").astype(jnp.int32)
    listing = items.reshape(top, rows).T
    listing = listing[jax.random.permutation(jax.random.fold_in(own, 1), rows)]
    offset_by = jax.random.randint(jax.random.fold_in(own, 2), (rows, 1), 0, top)
    return jnp.take_along_axis(listing, (jnp.arange(top)[None, :] + offset_by) % top, axis=1)


def portions_of(number_of, total, bound, slope, full):
    weights = [(1 << 20) // math.isqrt(grade ** slope) + 1 for grade in range(1, number_of + 1)]
    largest = bound if full else min(bound, max(-(-total // number_of), total * weights[0] // sum(weights)))
    least = 1 if total - largest >= number_of - 1 else 0
    given, spare = [largest] + [least] * (number_of - 1), total - largest - least * (number_of - 1)
    while spare > 0:
        movable = [i for i in range(1, number_of) if given[i] < largest] or [i for i in range(1, number_of) if given[i] < bound]
        whole, budget = sum([weights[i] for i in movable]), spare
        for i in movable:
            more = min(bound - given[i], max(1, budget * weights[i] // whole), spare)
            given[i] = given[i] + more
            spare = spare - more
    return np.array(given)


def noise(rng, extent, width, limit, pieces=(), kind=jnp.bfloat16):
    values = width * jax.random.normal(rng, extent, jnp.float32)
    if pieces:
        values = values * levels(rng, extent, pieces, -0.22, 0.18)
    return jnp.clip(values, -limit, limit).astype(kind)


def setup_inputs(seed: int = 0) -> dict:
    splits = jax.random.split(jax.random.key(seed), 8)
    tokens = noise(splits[0], (TOKENS, D), 1.0, 6.0, ((0, 32),))
    expert_ids_keys = jax.random.split(jax.random.fold_in(splits[1], 1), TOKENS // TOK_DEV)
    expert_ids_turns = jax.random.permutation(jax.random.fold_in(splits[1], 3), TOKENS // TOK_DEV)
    expert_ids = jax.vmap(lambda own, number: shared_out(jax.random.fold_in(splits[1], 2), own, number, TOK_DEV, EXPERTS, TOPK, CAP, 1))(expert_ids_keys, expert_ids_turns).reshape((TOKENS, TOPK))
    combine = jnp.clip(0.2 + 0.8 * jax.random.uniform(splits[2], (TOKENS, TOPK), jnp.float32) ** levels(splits[2], (TOKENS, TOPK), ((0, 32),), -0.2, 0.2), 0.2, 1.0)
    w_gate = noise(splits[3], (EXPERTS, D, H), D ** -0.5, 0.125, ((0, 16),))
    w_up = noise(splits[4], (EXPERTS, D, H), D ** -0.5, 0.125, ((0, 16),))
    w_down = noise(splits[5], (EXPERTS, H, D), H ** -0.5, 0.21875, ((0, 16),))
    grad_out = noise(splits[6], (TOKENS, D), 1.0, 6.0, ((0, 32),))
    return {"tokens": tokens, "expert_ids": expert_ids, "combine": combine, "w_gate": w_gate, "w_up": w_up, "w_down": w_down, "grad_out": grad_out}


def slot_table(ids):
    flat = ids.reshape(-1).astype(jnp.int32)
    onehot = (flat[:, None] == jnp.arange(EXPERTS, dtype=jnp.int32)[None, :]).astype(jnp.int32)
    ranks = jnp.sum(jnp.cumsum(onehot, axis=0) * onehot, axis=1) - 1
    return flat, ranks.astype(jnp.int32)


def expert_pass(rows, cotangent, w_gate, w_up, w_down):
    gate = jnp.dot(rows, w_gate, preferred_element_type=jnp.float32)
    upper = jnp.dot(rows, w_up, preferred_element_type=jnp.float32)
    sigma = jax.nn.sigmoid(gate)
    hidden = (gate * sigma * upper).astype(jnp.bfloat16)
    output = jnp.dot(hidden, w_down, preferred_element_type=jnp.float32).astype(jnp.bfloat16)
    d_hidden = lax.dot_general(cotangent, w_down, (((1,), (1,)), ((), ())), preferred_element_type=jnp.float32)
    d_gate = (d_hidden * upper * sigma * (1.0 + gate * (1.0 - sigma))).astype(jnp.bfloat16)
    d_upper = (d_hidden * gate * sigma).astype(jnp.bfloat16)
    d_rows = lax.dot_general(d_gate, w_gate, (((1,), (1,)), ((), ())), preferred_element_type=jnp.float32)
    d_rows = (d_rows + lax.dot_general(d_upper, w_up, (((1,), (1,)), ((), ())), preferred_element_type=jnp.float32)).astype(jnp.bfloat16)
    grad_g = lax.dot_general(rows, d_gate, (((0,), (0,)), ((), ())), preferred_element_type=jnp.float32).astype(jnp.bfloat16)
    grad_u = lax.dot_general(rows, d_upper, (((0,), (0,)), ((), ())), preferred_element_type=jnp.float32).astype(jnp.bfloat16)
    grad_d = lax.dot_general(hidden, cotangent, (((0,), (0,)), ((), ())), preferred_element_type=jnp.float32).astype(jnp.bfloat16)
    return output, d_rows, grad_g, grad_u, grad_d


def reference(tokens, expert_ids, combine, w_gate, w_up, w_down, grad_out):
    x_all = tokens.reshape(N_DP, N_EXPERT, TOK_DEV, D)
    id_all = expert_ids.reshape(N_DP, N_EXPERT, TOK_DEV, TOPK)
    c_all = combine.reshape(N_DP, N_EXPERT, TOK_DEV, TOPK)
    g_all = grad_out.reshape(N_DP, N_EXPERT, TOK_DEV, D)
    owners = jnp.arange(TOK_DEV * TOPK, dtype=jnp.int32) // TOPK

    def pack_source(x_dev, ids, c_dev, g_dev):
        flat, ranks = slot_table(ids)
        cot = (c_dev[:, :, None] * g_dev[:, None, :].astype(jnp.float32)).astype(jnp.bfloat16).reshape(TOK_DEV * TOPK, D)
        empty = jnp.zeros((EXPERTS, CAP, D), jnp.bfloat16)
        return empty.at[flat, ranks].set(x_dev[owners]), empty.at[flat, ranks].set(cot)

    def unpack_source(back, dback, ids, c_dev):
        flat, ranks = slot_table(ids)
        outs = back[flat, ranks].reshape(TOK_DEV, TOPK, D).astype(jnp.float32)
        drows = dback[flat, ranks].reshape(TOK_DEV, TOPK, D).astype(jnp.float32)
        mixed = jnp.sum(c_dev[:, :, None] * outs, axis=1).astype(jnp.bfloat16)
        return mixed, jnp.sum(drows, axis=1).astype(jnp.bfloat16)

    def one_expert(items):
        return expert_pass(*items)

    def one_row(totals, inputs):
        x_row, id_row, c_row, g_row = inputs
        sent_x, sent_c = jax.vmap(pack_source)(x_row, id_row, c_row, g_row)
        sent_x = jnp.swapaxes(sent_x, 0, 1).reshape(EXPERTS, N_EXPERT * CAP, D)
        sent_c = jnp.swapaxes(sent_c, 0, 1).reshape(EXPERTS, N_EXPERT * CAP, D)
        outs, drows, grad_g, grad_u, grad_d = lax.map(one_expert, (sent_x, sent_c, w_gate, w_up, w_down))
        outs = jnp.swapaxes(outs.reshape(EXPERTS, N_EXPERT, CAP, D), 0, 1)
        drows = jnp.swapaxes(drows.reshape(EXPERTS, N_EXPERT, CAP, D), 0, 1)
        mixed, grad_x = jax.vmap(unpack_source)(outs, drows, id_row, c_row)
        totals = (totals[0] + grad_g.astype(jnp.float32), totals[1] + grad_u.astype(jnp.float32), totals[2] + grad_d.astype(jnp.float32))
        return totals, (mixed, grad_x)

    start = (jnp.zeros((EXPERTS, D, H), jnp.float32), jnp.zeros((EXPERTS, D, H), jnp.float32), jnp.zeros((EXPERTS, H, D), jnp.float32))
    totals, (mixed, grad_x) = lax.scan(one_row, start, (x_all, id_all, c_all, g_all))
    return (mixed.reshape(TOKENS, D), grad_x.reshape(TOKENS, D), totals[0].astype(jnp.bfloat16), totals[1].astype(jnp.bfloat16), totals[2].astype(jnp.bfloat16))
```

```python
import functools

import jax
import jax.numpy as jnp
from jax import lax
from jax.sharding import PartitionSpec as P

def dot_nn(a, b):
    return jnp.dot(a, b, preferred_element_type=jnp.float32)


def dot_nt(a, b):
    return lax.dot_general(a, b, (((1,), (1,)), ((), ())), preferred_element_type=jnp.float32)


def dot_tn(a, b):
    return lax.dot_general(a, b, (((0,), (0,)), ((), ())), preferred_element_type=jnp.float32)


def weight_table(expert_ids, combine, n_experts):
    named = expert_ids[:, :, None] == jnp.arange(n_experts, dtype=jnp.int32)
    return jnp.sum(jnp.where(named, combine[:, :, None], 0.0), axis=1)


def on_device(wide, tokens, expert_ids, combine, w_gate, w_up, w_down, grad_out):
    n_experts = lax.axis_size("expert")
    d = lax.axis_index("dp")
    e = lax.axis_index("expert")
    width = tokens.shape[1]
    half = width // lax.axis_size("dp")
    own_rows = tokens.shape[0] * n_experts
    wg, wu, wd = w_gate[0], w_up[0], w_down[0]
    axes = ("dp", "expert") if wide else "expert"

    table_all = lax.all_gather(weight_table(expert_ids, combine, n_experts), axes, axis=0, tiled=True)
    x_all = lax.all_gather(tokens, axes, axis=0, tiled=True)
    g_all = lax.all_gather(grad_out, axes, axis=0, tiled=True)
    weight = lax.dynamic_slice_in_dim(table_all, e, 1, axis=1)

    def own(a):
        return lax.dynamic_slice_in_dim(a, d * own_rows, own_rows, axis=0) if wide else a

    def my_half(a):
        return lax.dynamic_slice_in_dim(a, d * half, half, axis=1) if wide else a

    gate = dot_nn(x_all, wg)
    upper = dot_nn(x_all, wu)
    sigma = jax.nn.sigmoid(gate)
    hidden = (gate * sigma * upper).astype(jnp.bfloat16)
    part = (own(weight) * dot_nn(own(hidden), wd)).astype(jnp.bfloat16)
    mixed = lax.psum_scatter(part, "expert", scatter_dimension=0, tiled=True)

    cotangent = (weight * g_all.astype(jnp.float32)).astype(jnp.bfloat16)
    d_hidden = dot_nt(cotangent, wd)
    d_gate = (d_hidden * upper * sigma * (1.0 + gate * (1.0 - sigma))).astype(jnp.bfloat16)
    d_upper = (d_hidden * gate * sigma).astype(jnp.bfloat16)
    d_rows = (dot_nt(own(d_gate), wg) + dot_nt(own(d_upper), wu)).astype(jnp.bfloat16)
    grad_tokens = lax.psum_scatter(d_rows, "expert", scatter_dimension=0, tiled=True)
    x_half = my_half(x_all)
    grad_g = dot_tn(x_half, d_gate).astype(jnp.bfloat16)
    grad_u = dot_tn(x_half, d_upper).astype(jnp.bfloat16)
    grad_d = dot_tn(hidden, my_half(cotangent)).astype(jnp.bfloat16)
    if not wide:
        grad_g = lax.psum_scatter(grad_g, "dp", scatter_dimension=0, tiled=True)
        grad_u = lax.psum_scatter(grad_u, "dp", scatter_dimension=0, tiled=True)
        grad_d = lax.psum_scatter(grad_d, "dp", scatter_dimension=1, tiled=True)
    return mixed, grad_tokens, grad_g[None], grad_u[None], grad_d[None]


def solution(mesh):
    rows = P(("dp", "expert"), None)
    expert = P("expert", None, None)
    return jax.shard_map(
        functools.partial(on_device, mesh.shape["dp"] == 2),
        mesh=mesh,
        in_specs=(rows, rows, rows, expert, expert, expert, rows),
        out_specs=(rows, rows, P("expert", "dp", None), P("expert", "dp", None), P("expert", None, "dp")),
        check_vma=False,
    )
```

```python
import jax
import jax.numpy as jnp
from jax import lax
from jax.experimental import pallas as pl
from jax.experimental.pallas import tpu as pltpu
from jax.sharding import PartitionSpec as P

def dot_nn(a, b):
    return jnp.dot(a, b, preferred_element_type=jnp.float32)


def dot_nt(a, b):
    return lax.dot_general(a, b, (((1,), (1,)), ((), ())), preferred_element_type=jnp.float32)


def dot_tn(a, b):
    return lax.dot_general(a, b, (((0,), (0,)), ((), ())), preferred_element_type=jnp.float32)


def weight_table(expert_ids, combine, n_experts):
    named = expert_ids[:, :, None] == jnp.arange(n_experts, dtype=jnp.int32)
    return jnp.sum(jnp.where(named, combine[:, :, None], 0.0), axis=1)


def on_device(tokens, expert_ids, combine, w_gate, w_up, w_down, grad_out):
    n_experts = lax.axis_size("expert")
    e = lax.axis_index("expert")
    wg, wu, wd = w_gate[0], w_up[0], w_down[0]

    table_all = lax.all_gather(weight_table(expert_ids, combine, n_experts), "expert", axis=0, tiled=True)
    x_all = lax.all_gather(tokens, "expert", axis=0, tiled=True)
    g_all = lax.all_gather(grad_out, "expert", axis=0, tiled=True)
    weight = lax.dynamic_slice_in_dim(table_all, e, 1, axis=1)

    gate = dot_nn(x_all, wg)
    upper = dot_nn(x_all, wu)
    sigma = jax.nn.sigmoid(gate)
    hidden = (gate * sigma * upper).astype(jnp.bfloat16)
    part = (weight * dot_nn(hidden, wd)).astype(jnp.bfloat16)
    mixed = lax.psum_scatter(part, "expert", scatter_dimension=0, tiled=True)

    cotangent = (weight * g_all.astype(jnp.float32)).astype(jnp.bfloat16)
    d_hidden = dot_nt(cotangent, wd)
    d_gate = (d_hidden * upper * sigma * (1.0 + gate * (1.0 - sigma))).astype(jnp.bfloat16)
    d_upper = (d_hidden * gate * sigma).astype(jnp.bfloat16)
    d_rows = (dot_nt(d_gate, wg) + dot_nt(d_upper, wu)).astype(jnp.bfloat16)
    grad_tokens = lax.psum_scatter(d_rows, "expert", scatter_dimension=0, tiled=True)
    grad_g = dot_tn(x_all, d_gate).astype(jnp.bfloat16)
    grad_u = dot_tn(x_all, d_upper).astype(jnp.bfloat16)
    grad_d = dot_tn(hidden, cotangent).astype(jnp.bfloat16)
    grad_g = lax.psum_scatter(grad_g, "dp", scatter_dimension=0, tiled=True)
    grad_u = lax.psum_scatter(grad_u, "dp", scatter_dimension=0, tiled=True)
    grad_d = lax.psum_scatter(grad_d, "dp", scatter_dimension=1, tiled=True)
    return mixed, grad_tokens, grad_g[None], grad_u[None], grad_d[None]


ROWS = 64
TILE = 256
Z, XD, YD, SD = 0, 3, 7, 15
LANES = 128


def fused_kernel(x_in, g_in, wg_hbm, wu_hbm, wd_hbm, mixed_out, gt_out, gg_out, gu_out, gd_out,
                 xs, gs, wg, wu, wd, hid, dg, du, part, s1, s2, s3,
                 wsem, send, recv, rsend, rrecv):
    width = g_in.shape[1]
    half = width // 2
    d = lax.axis_index("dp")
    e = lax.axis_index("expert")
    z, y, c = e // 4, (e // 2) % 2, e % 2

    def peer(rx, ry, rz, rc):
        return ((d + rx) % 2, (((z + rz) % 4) * 2 + (y + ry) % 2) * 2 + (c + rc) % 2)

    sibling, across_y, across_x = peer(0, 0, 0, 1), peer(0, 1, 0, 0), peer(1, 0, 0, 0)
    partners = [peer(0, 0, rz, 0) for rz in (1, 2, 3)] + [sibling, across_y, across_x]

    loads = [pltpu.make_async_copy(src, dst, wsem.at[i])
             for i, (src, dst) in enumerate(((wg_hbm, wg), (wu_hbm, wu), (wd_hbm, wd)))]
    for load in loads:
        load.start()
    barrier = pltpu.get_barrier_semaphore()
    for partner in partners:
        pl.semaphore_signal(barrier, inc=1, device_id=partner, device_id_type=pl.DeviceIdType.MESH)
    xs[0, 0:ROWS, :] = x_in[...]
    gs[0, 0:ROWS, :] = g_in[...]
    pl.semaphore_wait(barrier, len(partners))

    slots = (xs, gs)

    def shard(a, tile, rz):
        return slots[a].at[tile, pl.ds(rz * ROWS, ROWS)]

    def copy(a, src, dst, sem, device):
        return pltpu.make_async_remote_copy(
            src_ref=shard(a, *src), dst_ref=shard(a, *dst), send_sem=send.at[a, sem],
            recv_sem=recv.at[a, sem], device_id=device, device_id_type=pl.DeviceIdType.MESH)

    def along_z(a, rz):
        return copy(a, (0, 0), (0, 4 - rz), Z + 3 - rz, peer(0, 0, rz, 0))

    def along_y(a, rz):
        return copy(a, (0, rz), (2, rz), XD + rz, across_y)

    def along_x(a, ry, rz):
        return copy(a, (2 * ry, rz), (4 + 2 * ry, rz), YD + 4 * ry + rz, across_x)

    def to_core(a, rx, ry, rz):
        return copy(a, (4 * rx + 2 * ry, rz), (4 * rx + 2 * ry + 1, rz), SD + 8 * rx + 4 * ry + rz, sibling)

    for a in (0, 1):
        for rz in (2, 1, 3):
            along_z(a, rz).start()
        along_y(a, 0).start()
        along_x(a, 0, 0).start()
        to_core(a, 0, 0, 0).start()
    for a in (0, 1):
        for rz in (1, 3, 2):
            along_z(a, 4 - rz).wait_recv()
            along_y(a, rz).start()
            along_x(a, 0, rz).start()
            to_core(a, 0, 0, rz).start()
    for a in (0, 1):
        for rz in (0, 1, 3, 2):
            along_y(a, rz).wait_recv()
            along_x(a, 1, rz).start()
            to_core(a, 0, 1, rz).start()
    for load in loads:
        load.wait()

    lane = lax.broadcasted_iota(jnp.int32, (TILE, LANES), 1)
    mine = (lane < 48) & (lane % 16 == e)

    def tile_pass(tile, own):
        x = xs[tile, :, 0:width]
        side = xs[tile, :, width:width + LANES].astype(jnp.float32)
        weight = jnp.sum(jnp.where(mine, side, 0.0), axis=1, keepdims=True)
        gate = dot_nn(x, wg[...])
        upper = dot_nn(x, wu[...])
        sigma = jax.nn.sigmoid(gate)
        silu = gate * sigma
        hidden = (silu * upper * weight).astype(jnp.bfloat16)
        hid[tile] = hidden
        d_hidden = weight * dot_nt(gs[tile], wd[...])
        d_gate = (d_hidden * upper * sigma * (1.0 + gate * (1.0 - sigma))).astype(jnp.bfloat16)
        d_upper = (d_hidden * silu).astype(jnp.bfloat16)
        dg[tile] = d_gate
        du[tile] = d_upper
        if own:
            part[0, tile] = dot_nn(hidden, wd[...]).astype(jnp.bfloat16)
            part[1, tile] = (dot_nt(d_gate, wg[...]) + dot_nt(d_upper, wu[...])).astype(jnp.bfloat16)

    def chunk(rx, ry):
        for a in (0, 1):
            for rz in range(4):
                to_core(a, rx, ry, rz).wait_recv()
        first = 4 * rx + 2 * ry

        def step(i, carry):
            tile_pass(first + i, rx == 0)
            return carry

        lax.fori_loop(0, 2, step, 0)

    def rcopy(src, dst, a, sem, device):
        return pltpu.make_async_remote_copy(
            src_ref=src, dst_ref=dst, send_sem=rsend.at[a, sem], recv_sem=rrecv.at[a, sem],
            device_id=device, device_id_type=pl.DeviceIdType.MESH)

    def sum_core(a, ry):
        return rcopy(part.at[a, 2 * ry + 1], s1.at[a, ry], a, ry, sibling)

    def sum_y(a):
        return rcopy(part.at[a, 2], s2.at[a], a, 2, across_y)

    def sum_z(a, rz):
        return rcopy(part.at[a, 0, pl.ds(rz * ROWS, ROWS)], s3.at[a, 3 - rz], a, 2 + rz, peer(0, 0, rz, 0))

    def add(a, tile, other):
        total = part[a, tile].astype(jnp.float32) + other.astype(jnp.float32)
        part[a, tile] = total.astype(jnp.bfloat16)

    def from_x(ry):
        for a in (0, 1):
            for rz in (0, 1, 3, 2):
                along_x(a, ry, rz).wait_recv()
                to_core(a, 1, ry, rz).start()

    chunk(0, 0)
    for a in (0, 1):
        sum_core(a, 0).start()
    chunk(0, 1)
    for a in (0, 1):
        sum_core(a, 1).start()
    from_x(0)
    for a in (0, 1):
        sum_core(a, 1).wait_recv()
        add(a, 2, s1[a, 1])
        sum_y(a).start()
        sum_core(a, 0).wait_recv()
        add(a, 0, s1[a, 0])
    chunk(1, 0)
    for a in (0, 1):
        sum_y(a).wait_recv()
        add(a, 0, s2[a])
        for rz in (1, 2, 3):
            sum_z(a, rz).start()
    from_x(1)
    chunk(1, 1)

    def grads_in(j, carry):
        columns = pl.ds(pl.multiple_of(d * half + j * TILE, TILE), TILE)
        xt = xs[:, :, columns].reshape(8 * TILE, TILE).T
        rows = pl.ds(pl.multiple_of(j * TILE, TILE), TILE)
        gg_out[rows, :] = dot_nn(xt, dg[...].reshape(8 * TILE, -1)).astype(jnp.bfloat16)
        gu_out[rows, :] = dot_nn(xt, du[...].reshape(8 * TILE, -1)).astype(jnp.bfloat16)
        return carry

    lax.fori_loop(0, half // TILE, grads_in, 0)

    def grads_down(j, carry):
        columns = pl.ds(pl.multiple_of(j * TILE, TILE), TILE)
        ht = hid[:, :, columns].reshape(8 * TILE, TILE).T
        mine_half = pl.ds(pl.multiple_of(d * half, half), half)
        gd_out[columns, :] = dot_nn(ht, gs[:, :, mine_half].reshape(8 * TILE, half)).astype(jnp.bfloat16)
        return carry

    lax.fori_loop(0, hid.shape[2] // TILE, grads_down, 0)

    for a, out in ((0, mixed_out), (1, gt_out)):
        total = part[a, 0, 0:ROWS].astype(jnp.float32)
        for rz in (1, 2, 3):
            sum_z(a, rz).wait_recv()
        for i in range(3):
            total = total + s3[a, i].astype(jnp.float32)
        out[...] = total.astype(jnp.bfloat16)

    for a in (0, 1):
        for rz in (1, 2, 3):
            along_z(a, rz).wait_send()
            sum_z(a, rz).wait_send()
        for rz in range(4):
            along_y(a, rz).wait_send()
            for r in (0, 1):
                along_x(a, r, rz).wait_send()
                for rx in (0, 1):
                    to_core(a, rx, r, rz).wait_send()
        for r in (0, 1):
            sum_core(a, r).wait_send()
        sum_y(a).wait_send()


def fused_device(tokens, expert_ids, combine, w_gate, w_up, w_down, grad_out):
    tok, width = tokens.shape
    hidden = w_gate.shape[2]
    table = weight_table(expert_ids, combine, lax.axis_size("expert"))
    high = lax.reduce_precision(table, 8, 7)
    mid = lax.reduce_precision(table - high, 8, 7)
    side = jnp.concatenate([high, mid, table - high - mid], axis=1).astype(jnp.bfloat16)
    x = jnp.pad(jnp.concatenate([tokens, side], axis=1), ((0, ROWS - tok), (0, LANES - side.shape[1])))
    g = jnp.pad(grad_out, ((0, ROWS - tok), (0, 0)))
    bf16 = jnp.bfloat16
    vmem = pl.BlockSpec(memory_space=pltpu.VMEM)
    hbm = pl.BlockSpec(memory_space=pl.ANY)
    mixed, grad_tokens, grad_g, grad_u, grad_d = pl.pallas_call(
        fused_kernel,
        out_shape=[
            jax.ShapeDtypeStruct((ROWS, width), bf16),
            jax.ShapeDtypeStruct((ROWS, width), bf16),
            jax.ShapeDtypeStruct((width // 2, hidden), bf16),
            jax.ShapeDtypeStruct((width // 2, hidden), bf16),
            jax.ShapeDtypeStruct((hidden, width // 2), bf16),
        ],
        in_specs=[vmem, vmem, hbm, hbm, hbm],
        out_specs=[vmem] * 5,
        scratch_shapes=[
            pltpu.VMEM((8, TILE, width + LANES), bf16),
            pltpu.VMEM((8, TILE, width), bf16),
            pltpu.VMEM((width, hidden), bf16),
            pltpu.VMEM((width, hidden), bf16),
            pltpu.VMEM((hidden, width), bf16),
            pltpu.VMEM((8, TILE, hidden), bf16),
            pltpu.VMEM((8, TILE, hidden), bf16),
            pltpu.VMEM((8, TILE, hidden), bf16),
            pltpu.VMEM((2, 4, TILE, width), bf16),
            pltpu.VMEM((2, 2, TILE, width), bf16),
            pltpu.VMEM((2, TILE, width), bf16),
            pltpu.VMEM((2, 3, ROWS, width), bf16),
            pltpu.SemaphoreType.DMA((3,)),
            pltpu.SemaphoreType.DMA((2, 31)),
            pltpu.SemaphoreType.DMA((2, 31)),
            pltpu.SemaphoreType.DMA((2, 6)),
            pltpu.SemaphoreType.DMA((2, 6)),
        ],
        compiler_params=pltpu.CompilerParams(
            collective_id=0, has_side_effects=True, vmem_limit_bytes=63 * 1024 * 1024),
    )(x, g, w_gate[0], w_up[0], w_down[0])
    return mixed[:tok], grad_tokens[:tok], grad_g[None], grad_u[None], grad_d[None]


def solution(mesh):
    rows = P(("dp", "expert"), None)
    expert = P("expert", None, None)
    small = mesh.shape["dp"] == 2 and mesh.shape["expert"] == 16
    return jax.shard_map(
        fused_device if small else on_device,
        mesh=mesh,
        in_specs=(rows, rows, rows, expert, expert, expert, rows),
        out_specs=(rows, rows, P("expert", "dp", None), P("expert", "dp", None), P("expert", None, "dp")),
        check_vma=False,
    )
```

```python
import jax
import jax.numpy as jnp
from jax import lax
from jax.experimental import pallas as pl
from jax.experimental.pallas import tpu as pltpu
from jax.sharding import PartitionSpec as P

def dot_nn(a, b):
    return jnp.dot(a, b, preferred_element_type=jnp.float32)


def dot_nt(a, b):
    return lax.dot_general(a, b, (((1,), (1,)), ((), ())), preferred_element_type=jnp.float32)


def dot_tn(a, b):
    return lax.dot_general(a, b, (((0,), (0,)), ((), ())), preferred_element_type=jnp.float32)


def weight_table(expert_ids, combine, n_experts):
    named = expert_ids[:, :, None] == jnp.arange(n_experts, dtype=jnp.int32)
    return jnp.sum(jnp.where(named, combine[:, :, None], 0.0), axis=1)


def on_device(tokens, expert_ids, combine, w_gate, w_up, w_down, grad_out):
    n_experts = lax.axis_size("expert")
    e = lax.axis_index("expert")
    wg, wu, wd = w_gate[0], w_up[0], w_down[0]

    table_all = lax.all_gather(weight_table(expert_ids, combine, n_experts), "expert", axis=0, tiled=True)
    x_all = lax.all_gather(tokens, "expert", axis=0, tiled=True)
    g_all = lax.all_gather(grad_out, "expert", axis=0, tiled=True)
    weight = lax.dynamic_slice_in_dim(table_all, e, 1, axis=1)

    gate = dot_nn(x_all, wg)
    upper = dot_nn(x_all, wu)
    sigma = jax.nn.sigmoid(gate)
    hidden = (gate * sigma * upper).astype(jnp.bfloat16)
    part = (weight * dot_nn(hidden, wd)).astype(jnp.bfloat16)
    mixed = lax.psum_scatter(part, "expert", scatter_dimension=0, tiled=True)

    cotangent = (weight * g_all.astype(jnp.float32)).astype(jnp.bfloat16)
    d_hidden = dot_nt(cotangent, wd)
    d_gate = (d_hidden * upper * sigma * (1.0 + gate * (1.0 - sigma))).astype(jnp.bfloat16)
    d_upper = (d_hidden * gate * sigma).astype(jnp.bfloat16)
    d_rows = (dot_nt(d_gate, wg) + dot_nt(d_upper, wu)).astype(jnp.bfloat16)
    grad_tokens = lax.psum_scatter(d_rows, "expert", scatter_dimension=0, tiled=True)
    grad_g = dot_tn(x_all, d_gate).astype(jnp.bfloat16)
    grad_u = dot_tn(x_all, d_upper).astype(jnp.bfloat16)
    grad_d = dot_tn(hidden, cotangent).astype(jnp.bfloat16)
    grad_g = lax.psum_scatter(grad_g, "dp", scatter_dimension=0, tiled=True)
    grad_u = lax.psum_scatter(grad_u, "dp", scatter_dimension=0, tiled=True)
    grad_d = lax.psum_scatter(grad_d, "dp", scatter_dimension=1, tiled=True)
    return mixed, grad_tokens, grad_g[None], grad_u[None], grad_d[None]


ROWS = 64
TILE = 256
Z, XD, YD, SD = 0, 3, 7, 15
LANES = 128


def fused_kernel(x_in, g_in, wg_hbm, wu_hbm, wd_hbm, mixed_out, gt_out, gg_out, gu_out, gd_out,
                 xs, gs, wg, wu, wd, hid, dg, du, xhalf, ghalf, place, rows, part, s1, s2, s3,
                 wsem, send, recv, rsend, rrecv):
    width = g_in.shape[1]
    half = width // 2
    d = lax.axis_index("dp")
    e = lax.axis_index("expert")
    z, y, c = e // 4, (e // 2) % 2, e % 2

    def peer(rx, ry, rz, rc):
        return ((d + rx) % 2, (((z + rz) % 4) * 2 + (y + ry) % 2) * 2 + (c + rc) % 2)

    sibling, across_y, across_x = peer(0, 0, 0, 1), peer(0, 1, 0, 0), peer(1, 0, 0, 0)
    partners = [peer(0, 0, rz, 0) for rz in (1, 2, 3)] + [sibling, across_y, across_x]

    loads = [pltpu.make_async_copy(src, dst, wsem.at[i])
             for i, (src, dst) in enumerate(((wg_hbm, wg), (wu_hbm, wu), (wd_hbm, wd)))]
    for load in loads:
        load.start()
    barrier = pltpu.get_barrier_semaphore()
    for partner in partners:
        pl.semaphore_signal(barrier, inc=1, device_id=partner, device_id_type=pl.DeviceIdType.MESH)
    xs[0, 0:ROWS, :] = x_in[...]
    gs[0, 0:ROWS, :] = g_in[...]
    pl.semaphore_wait(barrier, len(partners))

    slots = (xs, gs)

    def shard(a, tile, rz):
        return slots[a].at[tile, pl.ds(rz * ROWS, ROWS)]

    def copy(a, src, dst, sem, device):
        return pltpu.make_async_remote_copy(
            src_ref=shard(a, *src), dst_ref=shard(a, *dst), send_sem=send.at[a, sem],
            recv_sem=recv.at[a, sem], device_id=device, device_id_type=pl.DeviceIdType.MESH)

    def along_z(a, rz):
        return copy(a, (0, 0), (0, 4 - rz), Z + 3 - rz, peer(0, 0, rz, 0))

    def along_y(a, rz):
        return copy(a, (0, rz), (2, rz), XD + rz, across_y)

    def along_x(a, ry, rz):
        return copy(a, (2 * ry, rz), (4 + 2 * ry, rz), YD + 4 * ry + rz, across_x)

    def to_core(a, rx, ry, rz):
        return copy(a, (4 * rx + 2 * ry, rz), (4 * rx + 2 * ry + 1, rz), SD + 8 * rx + 4 * ry + rz, sibling)

    for a in (0, 1):
        for rz in (2, 1, 3):
            along_z(a, rz).start()
        along_y(a, 0).start()
        along_x(a, 0, 0).start()
        to_core(a, 0, 0, 0).start()
    def from_z(a):
        for rz in (1, 3, 2):
            along_z(a, 4 - rz).wait_recv()
            along_y(a, rz).start()
            along_x(a, 0, rz).start()
            to_core(a, 0, 0, rz).start()

    def from_y(a):
        for rz in (0, 1, 3, 2):
            along_y(a, rz).wait_recv()
            along_x(a, 1, rz).start()
            to_core(a, 0, 1, rz).start()

    def from_x(a, ry):
        for rz in (0, 1, 3, 2):
            along_x(a, ry, rz).wait_recv()
            to_core(a, 1, ry, rz).start()

    lane = lax.broadcasted_iota(jnp.int32, (TILE, LANES), 1)
    mine = (lane < 48) & (lane % 16 == e)
    mine_half = pl.ds(pl.multiple_of(d * half, half), half)

    def weight_of(side):
        return jnp.sum(jnp.where(mine, side.astype(jnp.float32), 0.0), axis=1, keepdims=True)

    def packed(rc):
        return pl.ds(rc * LANES, LANES)

    def forward(rx, ry):
        chunk = 2 * rx + ry
        for rz in range(4):
            to_core(0, rx, ry, rz).wait_recv()
        first = lax.broadcasted_iota(jnp.int32, (TILE, TILE), 0)
        second = lax.broadcasted_iota(jnp.int32, (TILE, TILE), 1)
        upto = ((second <= first) & (second // ROWS == first // ROWS)).astype(jnp.float32).astype(jnp.bfloat16)
        base = (lax.broadcasted_iota(jnp.int32, (TILE, LANES), 0) // ROWS) * (LANES // 4)
        slot = (lane - base + 1).astype(jnp.float32)
        for rc in (0, 1):
            tile = 2 * chunk + rc
            weight = jnp.broadcast_to(weight_of(xs[tile, :, width:width + LANES]), (TILE, LANES))
            chosen = jnp.where(weight > 0.0, 1.0, 0.0)
            rank = dot_nn(upto, chosen.astype(jnp.bfloat16))
            table = jnp.where(rank == slot, chosen, 0.0).astype(jnp.bfloat16)
            place[tile] = table
            rows[packed(rc), :] = dot_nn(table.T, xs[tile]).astype(jnp.bfloat16)
        weight = weight_of(rows[:, width:width + LANES])
        xhalf[chunk] = rows[:, mine_half]
        gate = dot_nn(rows[:, 0:width], wg[...])
        upper = dot_nn(rows[:, 0:width], wu[...])
        sigma = jax.nn.sigmoid(gate)
        silu = gate * sigma * weight
        hidden = (silu * upper).astype(jnp.bfloat16)
        hid[chunk] = hidden
        dg[chunk] = (weight * upper * sigma * (1.0 + gate * (1.0 - sigma))).astype(jnp.bfloat16)
        du[chunk] = silu.astype(jnp.bfloat16)
        if rx == 0:
            out = dot_nn(hidden, wd[...]).astype(jnp.bfloat16)
            for rc in (0, 1):
                part[0, 2 * chunk + rc] = dot_nn(
                    place[2 * chunk + rc], out[rc * LANES:(rc + 1) * LANES]).astype(jnp.bfloat16)
            sum_core(0, ry).start()

    def backward(rx, ry):
        chunk = 2 * rx + ry
        for rz in range(4):
            to_core(1, rx, ry, rz).wait_recv()
        for rc in (0, 1):
            tile = 2 * chunk + rc
            rows[packed(rc), 0:width] = dot_nn(place[tile].T, gs[tile]).astype(jnp.bfloat16)
        ghalf[chunk] = rows[:, mine_half]
        d_hidden = dot_nt(rows[:, 0:width], wd[...])
        d_gate = (d_hidden * dg[chunk].astype(jnp.float32)).astype(jnp.bfloat16)
        d_upper = (d_hidden * du[chunk].astype(jnp.float32)).astype(jnp.bfloat16)
        dg[chunk] = d_gate
        du[chunk] = d_upper
        if rx == 0:
            out = (dot_nt(d_gate, wg[...]) + dot_nt(d_upper, wu[...])).astype(jnp.bfloat16)
            for rc in (0, 1):
                part[1, 2 * chunk + rc] = dot_nn(
                    place[2 * chunk + rc], out[rc * LANES:(rc + 1) * LANES]).astype(jnp.bfloat16)
            sum_core(1, ry).start()

    def rcopy(src, dst, a, sem, device):
        return pltpu.make_async_remote_copy(
            src_ref=src, dst_ref=dst, send_sem=rsend.at[a, sem], recv_sem=rrecv.at[a, sem],
            device_id=device, device_id_type=pl.DeviceIdType.MESH)

    def sum_core(a, ry):
        return rcopy(part.at[a, 2 * ry + 1], s1.at[a, ry], a, ry, sibling)

    def sum_y(a):
        return rcopy(part.at[a, 2], s2.at[a], a, 2, across_y)

    def sum_z(a, rz):
        return rcopy(part.at[a, 0, pl.ds(rz * ROWS, ROWS)], s3.at[a, 3 - rz], a, 2 + rz, peer(0, 0, rz, 0))

    def add(a, tile, other):
        total = part[a, tile].astype(jnp.float32) + other.astype(jnp.float32)
        part[a, tile] = total.astype(jnp.bfloat16)

    def sums_over_core(a):
        sum_core(a, 1).wait_recv()
        add(a, 2, s1[a, 1])
        sum_y(a).start()
        sum_core(a, 0).wait_recv()
        add(a, 0, s1[a, 0])

    def sums_over_y(a):
        sum_y(a).wait_recv()
        add(a, 0, s2[a])
        for rz in (1, 2, 3):
            sum_z(a, rz).start()

    from_z(0)
    for load in loads:
        load.wait()
    forward(0, 0)
    from_y(0)
    forward(0, 1)
    from_x(0, 0)
    sums_over_core(0)
    forward(1, 0)
    from_z(1)
    backward(0, 0)
    from_y(1)
    sums_over_y(0)
    from_x(0, 1)
    backward(0, 1)
    forward(1, 1)
    sums_over_core(1)
    from_x(1, 0)
    backward(1, 0)
    sums_over_y(1)
    from_x(1, 1)
    backward(1, 1)

    packed_rows = 4 * TILE

    def grads_in(j, carry):
        block = pl.ds(pl.multiple_of(j * 512, 512), 512)
        xt = xhalf[:, :, block].reshape(packed_rows, 512).T
        gg_out[block, :] = dot_nn(xt, dg[...].reshape(packed_rows, -1)).astype(jnp.bfloat16)
        gu_out[block, :] = dot_nn(xt, du[...].reshape(packed_rows, -1)).astype(jnp.bfloat16)
        return carry

    lax.fori_loop(0, half // 512, grads_in, 0)

    def grads_down(j, carry):
        block = pl.ds(pl.multiple_of(j * 384, 384), 384)
        ht = hid[:, :, block].reshape(packed_rows, 384).T
        gd_out[block, :] = dot_nn(ht, ghalf[...].reshape(packed_rows, half)).astype(jnp.bfloat16)
        return carry

    lax.fori_loop(0, hid.shape[2] // 384, grads_down, 0)

    for a, out in ((0, mixed_out), (1, gt_out)):
        total = part[a, 0, 0:ROWS].astype(jnp.float32)
        for rz in (1, 2, 3):
            sum_z(a, rz).wait_recv()
        for i in range(3):
            total = total + s3[a, i].astype(jnp.float32)
        out[...] = total.astype(jnp.bfloat16)

    for a in (0, 1):
        for rz in (1, 2, 3):
            along_z(a, rz).wait_send()
            sum_z(a, rz).wait_send()
        for rz in range(4):
            along_y(a, rz).wait_send()
            for r in (0, 1):
                along_x(a, r, rz).wait_send()
                for rx in (0, 1):
                    to_core(a, rx, r, rz).wait_send()
        for r in (0, 1):
            sum_core(a, r).wait_send()
        sum_y(a).wait_send()


def fused_device(tokens, expert_ids, combine, w_gate, w_up, w_down, grad_out):
    tok, width = tokens.shape
    hidden = w_gate.shape[2]
    table = weight_table(expert_ids, combine, lax.axis_size("expert"))
    high = lax.reduce_precision(table, 8, 7)
    mid = lax.reduce_precision(table - high, 8, 7)
    side = jnp.concatenate([high, mid, table - high - mid], axis=1).astype(jnp.bfloat16)
    x = jnp.pad(jnp.concatenate([tokens, side], axis=1), ((0, ROWS - tok), (0, LANES - side.shape[1])))
    g = jnp.pad(grad_out, ((0, ROWS - tok), (0, 0)))
    bf16 = jnp.bfloat16
    vmem = pl.BlockSpec(memory_space=pltpu.VMEM)
    hbm = pl.BlockSpec(memory_space=pl.ANY)
    mixed, grad_tokens, grad_g, grad_u, grad_d = pl.pallas_call(
        fused_kernel,
        out_shape=[
            jax.ShapeDtypeStruct((ROWS, width), bf16),
            jax.ShapeDtypeStruct((ROWS, width), bf16),
            jax.ShapeDtypeStruct((width // 2, hidden), bf16),
            jax.ShapeDtypeStruct((width // 2, hidden), bf16),
            jax.ShapeDtypeStruct((hidden, width // 2), bf16),
        ],
        in_specs=[vmem, vmem, hbm, hbm, hbm],
        out_specs=[vmem] * 5,
        scratch_shapes=[
            pltpu.VMEM((8, TILE, width + LANES), bf16),
            pltpu.VMEM((8, TILE, width), bf16),
            pltpu.VMEM((width, hidden), bf16),
            pltpu.VMEM((width, hidden), bf16),
            pltpu.VMEM((hidden, width), bf16),
            pltpu.VMEM((4, TILE, hidden), bf16),
            pltpu.VMEM((4, TILE, hidden), bf16),
            pltpu.VMEM((4, TILE, hidden), bf16),
            pltpu.VMEM((4, TILE, width // 2), bf16),
            pltpu.VMEM((4, TILE, width // 2), bf16),
            pltpu.VMEM((8, TILE, LANES), bf16),
            pltpu.VMEM((TILE, width + LANES), bf16),
            pltpu.VMEM((2, 4, TILE, width), bf16),
            pltpu.VMEM((2, 2, TILE, width), bf16),
            pltpu.VMEM((2, TILE, width), bf16),
            pltpu.VMEM((2, 3, ROWS, width), bf16),
            pltpu.SemaphoreType.DMA((3,)),
            pltpu.SemaphoreType.DMA((2, 31)),
            pltpu.SemaphoreType.DMA((2, 31)),
            pltpu.SemaphoreType.DMA((2, 6)),
            pltpu.SemaphoreType.DMA((2, 6)),
        ],
        compiler_params=pltpu.CompilerParams(
            collective_id=0, has_side_effects=True, vmem_limit_bytes=63 * 1024 * 1024),
    )(x, g, w_gate[0], w_up[0], w_down[0])
    return mixed[:tok], grad_tokens[:tok], grad_g[None], grad_u[None], grad_d[None]


def solution(mesh):
    rows = P(("dp", "expert"), None)
    expert = P("expert", None, None)
    small = mesh.shape["dp"] == 2 and mesh.shape["expert"] == 16
    return jax.shard_map(
        fused_device if small else on_device,
        mesh=mesh,
        in_specs=(rows, rows, rows, expert, expert, expert, rows),
        out_specs=(rows, rows, P("expert", "dp", None), P("expert", "dp", None), P("expert", None, "dp")),
        check_vma=False,
    )
```

```python
import jax
import jax.numpy as jnp
from jax import lax
from jax.experimental import pallas as pl
from jax.experimental.pallas import tpu as pltpu
from jax.sharding import PartitionSpec as P

def dot_nn(a, b):
    return jnp.dot(a, b, preferred_element_type=jnp.float32)


def dot_nt(a, b):
    return lax.dot_general(a, b, (((1,), (1,)), ((), ())), preferred_element_type=jnp.float32)


def dot_tn(a, b):
    return lax.dot_general(a, b, (((0,), (0,)), ((), ())), preferred_element_type=jnp.float32)


def weight_table(expert_ids, combine, n_experts):
    named = expert_ids[:, :, None] == jnp.arange(n_experts, dtype=jnp.int32)
    return jnp.sum(jnp.where(named, combine[:, :, None], 0.0), axis=1)


def on_device(tokens, expert_ids, combine, w_gate, w_up, w_down, grad_out):
    n_experts = lax.axis_size("expert")
    e = lax.axis_index("expert")
    wg, wu, wd = w_gate[0], w_up[0], w_down[0]

    table_all = lax.all_gather(weight_table(expert_ids, combine, n_experts), "expert", axis=0, tiled=True)
    x_all = lax.all_gather(tokens, "expert", axis=0, tiled=True)
    g_all = lax.all_gather(grad_out, "expert", axis=0, tiled=True)
    weight = lax.dynamic_slice_in_dim(table_all, e, 1, axis=1)

    gate = dot_nn(x_all, wg)
    upper = dot_nn(x_all, wu)
    sigma = jax.nn.sigmoid(gate)
    hidden = (gate * sigma * upper).astype(jnp.bfloat16)
    part = (weight * dot_nn(hidden, wd)).astype(jnp.bfloat16)
    mixed = lax.psum_scatter(part, "expert", scatter_dimension=0, tiled=True)

    cotangent = (weight * g_all.astype(jnp.float32)).astype(jnp.bfloat16)
    d_hidden = dot_nt(cotangent, wd)
    d_gate = (d_hidden * upper * sigma * (1.0 + gate * (1.0 - sigma))).astype(jnp.bfloat16)
    d_upper = (d_hidden * gate * sigma).astype(jnp.bfloat16)
    d_rows = (dot_nt(d_gate, wg) + dot_nt(d_upper, wu)).astype(jnp.bfloat16)
    grad_tokens = lax.psum_scatter(d_rows, "expert", scatter_dimension=0, tiled=True)
    grad_g = dot_tn(x_all, d_gate).astype(jnp.bfloat16)
    grad_u = dot_tn(x_all, d_upper).astype(jnp.bfloat16)
    grad_d = dot_tn(hidden, cotangent).astype(jnp.bfloat16)
    grad_g = lax.psum_scatter(grad_g, "dp", scatter_dimension=0, tiled=True)
    grad_u = lax.psum_scatter(grad_u, "dp", scatter_dimension=0, tiled=True)
    grad_d = lax.psum_scatter(grad_d, "dp", scatter_dimension=1, tiled=True)
    return mixed, grad_tokens, grad_g[None], grad_u[None], grad_d[None]


ROWS = (64, 48)
TAIL = 8
TILE = 256
Z, XD, YD, SD = 0, 3, 7, 15
LANES = 128


def fused_kernel(x_in, side_in, g_in, wg_hbm, wu_hbm, wd_hbm, mixed_out, gt_out, gg_out, gu_out, gd_out,
                 xs, gs, wg, wu, wd, hid, dg, du, xhalf, ghalf, place, rows, part, s1, s2, s3,
                 wsem, send, recv, rsend, rrecv):
    width = g_in.shape[1]
    half = width // 2
    d = lax.axis_index("dp")
    e = lax.axis_index("expert")
    z, y, c = e // 4, (e // 2) % 2, e % 2

    def peer(rx, ry, rz, rc):
        return ((d + rx) % 2, (((z + rz) % 4) * 2 + (y + ry) % 2) * 2 + (c + rc) % 2)

    sibling, across_y, across_x = peer(0, 0, 0, 1), peer(0, 1, 0, 0), peer(1, 0, 0, 0)
    partners = [peer(0, 0, rz, 0) for rz in (1, 2, 3)] + [sibling, across_y, across_x]

    loads = [pltpu.make_async_copy(src, dst, wsem.at[i])
             for i, (src, dst) in enumerate(((wg_hbm, wg), (wu_hbm, wu), (wd_hbm, wd)))]
    for load in loads:
        load.start()
    barrier = pltpu.get_barrier_semaphore()
    for partner in partners:
        pl.semaphore_signal(barrier, inc=1, device_id=partner, device_id_type=pl.DeviceIdType.MESH)
    tok = x_in.shape[0]
    xs[0, 0:ROWS[0], 0:width] = jnp.concatenate(
        [x_in[...].astype(jnp.float32), g_in[ROWS[1]:tok, :].astype(jnp.float32)], axis=0).astype(jnp.bfloat16)
    xs[0, 0:ROWS[0], width:width + LANES] = side_in[...]
    gs[0, 0:ROWS[1], :] = g_in[0:ROWS[1], :]
    pl.semaphore_wait(barrier, len(partners))

    slots = (xs, gs)

    def shard(a, tile, rz):
        return slots[a].at[tile, pl.ds(rz * ROWS[a], ROWS[a])]

    def copy(a, src, dst, sem, device):
        return pltpu.make_async_remote_copy(
            src_ref=shard(a, *src), dst_ref=shard(a, *dst), send_sem=send.at[a, sem],
            recv_sem=recv.at[a, sem], device_id=device, device_id_type=pl.DeviceIdType.MESH)

    def along_z(a, rz):
        return copy(a, (0, 0), (0, 4 - rz), Z + 3 - rz, peer(0, 0, rz, 0))

    def along_y(a, rz):
        return copy(a, (0, rz), (2, rz), XD + rz, across_y)

    def along_x(a, ry, rz):
        return copy(a, (2 * ry, rz), (4 + 2 * ry, rz), YD + 4 * ry + rz, across_x)

    def to_core(a, rx, ry, rz):
        return copy(a, (4 * rx + 2 * ry, rz), (4 * rx + 2 * ry + 1, rz), SD + 8 * rx + 4 * ry + rz, sibling)

    for a in (0, 1):
        for rz in (2, 1, 3):
            along_z(a, rz).start()
        along_y(a, 0).start()
        along_x(a, 0, 0).start()
        to_core(a, 0, 0, 0).start()
    def from_z(a):
        for rz in (1, 3, 2):
            along_z(a, 4 - rz).wait_recv()
            along_y(a, rz).start()
            along_x(a, 0, rz).start()
            to_core(a, 0, 0, rz).start()

    def from_y(a):
        for rz in (0, 1, 3, 2):
            along_y(a, rz).wait_recv()
            along_x(a, 1, rz).start()
            to_core(a, 0, 1, rz).start()

    def from_x(a, ry):
        for rz in (0, 1, 3, 2):
            along_x(a, ry, rz).wait_recv()
            to_core(a, 1, ry, rz).start()

    lane = lax.broadcasted_iota(jnp.int32, (TILE, LANES), 1)
    mine_half = pl.ds(pl.multiple_of(d * half, half), half)

    def weight_of(side):
        at = lax.broadcasted_iota(jnp.int32, side.shape, 1)
        mine = (at < 48) & (at % 16 == e)
        return jnp.sum(jnp.where(mine, side.astype(jnp.float32), 0.0), axis=1, keepdims=True)

    def packed(i):
        return pl.ds(i * LANES, LANES)

    def forward(rx):
        first = lax.broadcasted_iota(jnp.int32, (TILE, TILE), 0)
        second = lax.broadcasted_iota(jnp.int32, (TILE, TILE), 1)
        upto = ((second <= first) & (second // 64 == first // 64)).astype(jnp.float32).astype(jnp.bfloat16)
        base = (lax.broadcasted_iota(jnp.int32, (TILE, LANES), 0) // 64) * (LANES // 4)
        slot = (lane - base + 1).astype(jnp.float32)
        for i in range(4):
            for rz in range(4 * (i % 2)):
                to_core(0, rx, i // 2, rz).wait_recv()
            tile = 4 * rx + i
            weight = jnp.broadcast_to(weight_of(xs[tile, :, width:width + LANES]), (TILE, LANES))
            chosen = jnp.where(weight > 0.0, 1.0, 0.0)
            rank = dot_nn(upto, chosen.astype(jnp.bfloat16))
            table = jnp.where(rank == slot, chosen, 0.0).astype(jnp.bfloat16)
            place[tile] = table
            rows[packed(i), :] = dot_nn(table.T, xs[tile]).astype(jnp.bfloat16)
        weight = weight_of(rows[:, width:width + LANES])
        xhalf[rx] = rows[:, mine_half]
        for h in range(hid.shape[2] // TILE):
            cols = pl.ds(h * TILE, TILE)
            gate = dot_nn(rows[:, 0:width], wg[:, cols])
            upper = dot_nn(rows[:, 0:width], wu[:, cols])
            sigma = jax.nn.sigmoid(gate)
            silu = gate * sigma * weight
            hid[rx, :, cols] = (silu * upper).astype(jnp.bfloat16)
            dg[rx, :, cols] = (weight * upper * sigma * (1.0 + gate * (1.0 - sigma))).astype(jnp.bfloat16)
            du[rx, :, cols] = silu.astype(jnp.bfloat16)
        if rx == 0:
            spread(0, lambda cols: dot_nn(hid[0], wd[:, cols]))

    def spread(a, product):
        for n in range(width // 512):
            cols = pl.ds(n * 512, 512)
            out = product(cols).astype(jnp.bfloat16)
            for i in range(4):
                part[a, i, :, cols] = dot_nn(place[i], out[i * LANES:(i + 1) * LANES]).astype(jnp.bfloat16)
        for ry in (0, 1):
            sum_core(a, ry).start()

    def backward(rx):
        for i in range(4):
            for rz in range(4 * (i % 2)):
                to_core(1, rx, i // 2, rz).wait_recv()
            tile = 4 * rx + i
            table = place[tile].astype(jnp.float32)
            blank = jnp.zeros((TAIL, LANES), jnp.float32)
            heads = [table[64 * rz:64 * rz + 48] for rz in range(4)]
            tails = [t for rz in range(4) for t in (blank, table[64 * rz + 48:64 * rz + 56])]
            table = jnp.concatenate(heads + tails, axis=0).astype(jnp.bfloat16)
            grads = jnp.concatenate(
                [gs[tile]] + [xs[tile, 64 * rz + 48:64 * rz + 64, 0:width] for rz in range(4)], axis=0)
            rows[packed(i), 0:width] = dot_nn(table.T, grads).astype(jnp.bfloat16)
        ghalf[rx] = rows[:, mine_half]
        for h in range(hid.shape[2] // TILE):
            cols = pl.ds(h * TILE, TILE)
            d_hidden = dot_nt(rows[:, 0:width], wd[cols, :])
            dg[rx, :, cols] = (d_hidden * dg[rx, :, cols].astype(jnp.float32)).astype(jnp.bfloat16)
            du[rx, :, cols] = (d_hidden * du[rx, :, cols].astype(jnp.float32)).astype(jnp.bfloat16)
        if rx == 0:
            spread(1, lambda cols: dot_nt(dg[0], wg[cols, :]) + dot_nt(du[0], wu[cols, :]))

    def rcopy(src, dst, a, sem, device):
        return pltpu.make_async_remote_copy(
            src_ref=src, dst_ref=dst, send_sem=rsend.at[a, sem], recv_sem=rrecv.at[a, sem],
            device_id=device, device_id_type=pl.DeviceIdType.MESH)

    def sum_core(a, ry):
        return rcopy(part.at[a, 2 * ry + 1], s1.at[a, ry], a, ry, sibling)

    def sum_y(a):
        return rcopy(part.at[a, 2], s2.at[a], a, 2, across_y)

    def sum_z(a, rz):
        return rcopy(part.at[a, 0, pl.ds(rz * ROWS[0], ROWS[0])], s3.at[a, 3 - rz], a, 2 + rz, peer(0, 0, rz, 0))

    def add(a, tile, other):
        total = part[a, tile].astype(jnp.float32) + other.astype(jnp.float32)
        part[a, tile] = total.astype(jnp.bfloat16)

    def sums_over_core(a):
        sum_core(a, 1).wait_recv()
        add(a, 2, s1[a, 1])
        sum_y(a).start()
        sum_core(a, 0).wait_recv()
        add(a, 0, s1[a, 0])

    def sums_over_y(a):
        sum_y(a).wait_recv()
        add(a, 0, s2[a])
        for rz in (1, 2, 3):
            sum_z(a, rz).start()

    from_z(0)
    from_y(0)
    for load in loads:
        load.wait()
    forward(0)
    from_x(0, 0)
    from_z(1)
    sums_over_core(0)
    from_y(1)
    from_x(0, 1)
    backward(0)
    sums_over_y(0)
    from_x(1, 0)
    forward(1)
    sums_over_core(1)
    from_x(1, 1)
    sums_over_y(1)
    backward(1)

    packed_rows = 4 * TILE

    def grads_in(j, carry):
        block = pl.ds(pl.multiple_of(j * 512, 512), 512)
        xt = xhalf[:, :, block].reshape(packed_rows, 512).T
        gg_out[block, :] = dot_nn(xt, dg[...].reshape(packed_rows, -1)).astype(jnp.bfloat16)
        gu_out[block, :] = dot_nn(xt, du[...].reshape(packed_rows, -1)).astype(jnp.bfloat16)
        return carry

    lax.fori_loop(0, half // 512, grads_in, 0)

    def grads_down(j, carry):
        block = pl.ds(pl.multiple_of(j * 384, 384), 384)
        ht = hid[:, :, block].reshape(packed_rows, 384).T
        gd_out[block, :] = dot_nn(ht, ghalf[...].reshape(packed_rows, half)).astype(jnp.bfloat16)
        return carry

    lax.fori_loop(0, hid.shape[2] // 384, grads_down, 0)

    for a, out in ((0, mixed_out), (1, gt_out)):
        total = part[a, 0, 0:ROWS[0]].astype(jnp.float32)
        for rz in (1, 2, 3):
            sum_z(a, rz).wait_recv()
        for i in range(3):
            total = total + s3[a, i].astype(jnp.float32)
        out[...] = total[0:tok].astype(jnp.bfloat16)

    for a in (0, 1):
        for rz in (1, 2, 3):
            along_z(a, rz).wait_send()
            sum_z(a, rz).wait_send()
        for rz in range(4):
            along_y(a, rz).wait_send()
            for r in (0, 1):
                along_x(a, r, rz).wait_send()
                for rx in (0, 1):
                    to_core(a, rx, r, rz).wait_send()
        for r in (0, 1):
            sum_core(a, r).wait_send()
        sum_y(a).wait_send()


def fused_device(tokens, expert_ids, combine, w_gate, w_up, w_down, grad_out):
    tok, width = tokens.shape
    hidden = w_gate.shape[2]
    table = weight_table(expert_ids, combine, lax.axis_size("expert"))
    high = lax.reduce_precision(table, 8, 7)
    mid = lax.reduce_precision(table - high, 8, 7)
    side = jnp.concatenate([high, mid, table - high - mid], axis=1).astype(jnp.bfloat16)
    side = jnp.pad(side, ((0, ROWS[0] - tok), (0, LANES - side.shape[1])))
    bf16 = jnp.bfloat16
    vmem = pl.BlockSpec(memory_space=pltpu.VMEM)
    hbm = pl.BlockSpec(memory_space=pl.ANY)
    mixed, grad_tokens, grad_g, grad_u, grad_d = pl.pallas_call(
        fused_kernel,
        out_shape=[
            jax.ShapeDtypeStruct((tok, width), bf16),
            jax.ShapeDtypeStruct((tok, width), bf16),
            jax.ShapeDtypeStruct((width // 2, hidden), bf16),
            jax.ShapeDtypeStruct((width // 2, hidden), bf16),
            jax.ShapeDtypeStruct((hidden, width // 2), bf16),
        ],
        in_specs=[vmem, vmem, vmem, hbm, hbm, hbm],
        out_specs=[vmem] * 5,
        scratch_shapes=[
            pltpu.VMEM((8, TILE, width + LANES), bf16),
            pltpu.VMEM((8, 4 * ROWS[1], width), bf16),
            pltpu.VMEM((width, hidden), bf16),
            pltpu.VMEM((width, hidden), bf16),
            pltpu.VMEM((hidden, width), bf16),
            pltpu.VMEM((2, 2 * TILE, hidden), bf16),
            pltpu.VMEM((2, 2 * TILE, hidden), bf16),
            pltpu.VMEM((2, 2 * TILE, hidden), bf16),
            pltpu.VMEM((2, 2 * TILE, width // 2), bf16),
            pltpu.VMEM((2, 2 * TILE, width // 2), bf16),
            pltpu.VMEM((8, TILE, LANES), bf16),
            pltpu.VMEM((2 * TILE, width + LANES), bf16),
            pltpu.VMEM((2, 4, TILE, width), bf16),
            pltpu.VMEM((2, 2, TILE, width), bf16),
            pltpu.VMEM((2, TILE, width), bf16),
            pltpu.VMEM((2, 3, ROWS[0], width), bf16),
            pltpu.SemaphoreType.DMA((3,)),
            pltpu.SemaphoreType.DMA((2, 31)),
            pltpu.SemaphoreType.DMA((2, 31)),
            pltpu.SemaphoreType.DMA((2, 6)),
            pltpu.SemaphoreType.DMA((2, 6)),
        ],
        compiler_params=pltpu.CompilerParams(
            collective_id=0, has_side_effects=True, vmem_limit_bytes=63 * 1024 * 1024),
    )(tokens, side, grad_out, w_gate[0], w_up[0], w_down[0])
    return mixed, grad_tokens, grad_g[None], grad_u[None], grad_d[None]


def solution(mesh):
    rows = P(("dp", "expert"), None)
    expert = P("expert", None, None)
    small = mesh.shape["dp"] == 2 and mesh.shape["expert"] == 16
    return jax.shard_map(
        fused_device if small else on_device,
        mesh=mesh,
        in_specs=(rows, rows, rows, expert, expert, expert, rows),
        out_specs=(rows, rows, P("expert", "dp", None), P("expert", "dp", None), P("expert", None, "dp")),
        check_vma=False,
    )
```

```python
import jax
import jax.numpy as jnp
from jax import lax
from jax.experimental import pallas as pl
from jax.experimental.pallas import tpu as pltpu
from jax.sharding import PartitionSpec as P

def dot_nn(a, b):
    return jnp.dot(a, b, preferred_element_type=jnp.float32)


def dot_nt(a, b):
    return lax.dot_general(a, b, (((1,), (1,)), ((), ())), preferred_element_type=jnp.float32)


def dot_tn(a, b):
    return lax.dot_general(a, b, (((0,), (0,)), ((), ())), preferred_element_type=jnp.float32)


def weight_table(expert_ids, combine, n_experts):
    named = expert_ids[:, :, None] == jnp.arange(n_experts, dtype=jnp.int32)
    return jnp.sum(jnp.where(named, combine[:, :, None], 0.0), axis=1)


def on_device(tokens, expert_ids, combine, w_gate, w_up, w_down, grad_out):
    n_experts = lax.axis_size("expert")
    e = lax.axis_index("expert")
    wg, wu, wd = w_gate[0], w_up[0], w_down[0]

    table_all = lax.all_gather(weight_table(expert_ids, combine, n_experts), "expert", axis=0, tiled=True)
    x_all = lax.all_gather(tokens, "expert", axis=0, tiled=True)
    g_all = lax.all_gather(grad_out, "expert", axis=0, tiled=True)
    weight = lax.dynamic_slice_in_dim(table_all, e, 1, axis=1)

    gate = dot_nn(x_all, wg)
    upper = dot_nn(x_all, wu)
    sigma = jax.nn.sigmoid(gate)
    hidden = (gate * sigma * upper).astype(jnp.bfloat16)
    part = (weight * dot_nn(hidden, wd)).astype(jnp.bfloat16)
    mixed = lax.psum_scatter(part, "expert", scatter_dimension=0, tiled=True)

    cotangent = (weight * g_all.astype(jnp.float32)).astype(jnp.bfloat16)
    d_hidden = dot_nt(cotangent, wd)
    d_gate = (d_hidden * upper * sigma * (1.0 + gate * (1.0 - sigma))).astype(jnp.bfloat16)
    d_upper = (d_hidden * gate * sigma).astype(jnp.bfloat16)
    d_rows = (dot_nt(d_gate, wg) + dot_nt(d_upper, wu)).astype(jnp.bfloat16)
    grad_tokens = lax.psum_scatter(d_rows, "expert", scatter_dimension=0, tiled=True)
    grad_g = dot_tn(x_all, d_gate).astype(jnp.bfloat16)
    grad_u = dot_tn(x_all, d_upper).astype(jnp.bfloat16)
    grad_d = dot_tn(hidden, cotangent).astype(jnp.bfloat16)
    grad_g = lax.psum_scatter(grad_g, "dp", scatter_dimension=0, tiled=True)
    grad_u = lax.psum_scatter(grad_u, "dp", scatter_dimension=0, tiled=True)
    grad_d = lax.psum_scatter(grad_d, "dp", scatter_dimension=1, tiled=True)
    return mixed, grad_tokens, grad_g[None], grad_u[None], grad_d[None]


ROWS = (64, 48)
TAIL = 8
TILE = 256
Z, XD, YD, SD = 0, 3, 7, 15
LANES = 128


def fused_kernel(x_in, side_in, g_in, wg_hbm, wu_hbm, wd_hbm, mixed_out, gt_out, gg_out, gu_out, gd_out,
                 xs, gs, wg, wu, wd, hid, dg, du, xhalf, ghalf, place, rows, part, s1, s2, s3,
                 wsem, send, recv, rsend, rrecv):
    width = g_in.shape[1]
    half = width // 2
    d = lax.axis_index("dp")
    e = lax.axis_index("expert")
    z, y, c = e // 4, (e // 2) % 2, e % 2

    def peer(rx, ry, rz, rc):
        return ((d + rx) % 2, (((z + rz) % 4) * 2 + (y + ry) % 2) * 2 + (c + rc) % 2)

    sibling, across_y, across_x = peer(0, 0, 0, 1), peer(0, 1, 0, 0), peer(1, 0, 0, 0)
    partners = [peer(0, 0, rz, 0) for rz in (1, 2, 3)] + [sibling, across_y, across_x]

    loads = [pltpu.make_async_copy(src, dst, wsem.at[i])
             for i, (src, dst) in enumerate(((wg_hbm, wg), (wu_hbm, wu), (wd_hbm, wd)))]
    for load in loads:
        load.start()
    barrier = pltpu.get_barrier_semaphore()
    for partner in partners:
        pl.semaphore_signal(barrier, inc=1, device_id=partner, device_id_type=pl.DeviceIdType.MESH)
    tok = x_in.shape[0]
    xs[0, 0:ROWS[0], 0:width] = jnp.concatenate(
        [x_in[...].astype(jnp.float32), g_in[ROWS[1]:tok, :].astype(jnp.float32)], axis=0).astype(jnp.bfloat16)
    xs[0, 0:ROWS[0], width:width + LANES] = side_in[...]
    gs[0, 0:ROWS[1], :] = g_in[0:ROWS[1], :]
    pl.semaphore_wait(barrier, len(partners))

    slots = (xs, gs)

    def shard(a, tile, rz):
        return slots[a].at[tile, pl.ds(rz * ROWS[a], ROWS[a])]

    def copy(a, src, dst, sem, device):
        return pltpu.make_async_remote_copy(
            src_ref=shard(a, *src), dst_ref=shard(a, *dst), send_sem=send.at[a, sem],
            recv_sem=recv.at[a, sem], device_id=device, device_id_type=pl.DeviceIdType.MESH)

    def along_z(a, rz):
        return copy(a, (0, 0), (0, 4 - rz), Z + 3 - rz, peer(0, 0, rz, 0))

    def along_y(a, rz):
        return copy(a, (0, rz), (2, rz), XD + rz, across_y)

    def along_x(a, ry, rz):
        return copy(a, (2 * ry, rz), (4 + 2 * ry, rz), YD + 4 * ry + rz, across_x)

    def to_core(a, rx, ry, rz):
        return copy(a, (4 * rx + 2 * ry, rz), (4 * rx + 2 * ry + 1, rz), SD + 8 * rx + 4 * ry + rz, sibling)

    for a in (0, 1):
        for rz in (2, 1, 3):
            along_z(a, rz).start()
        along_y(a, 0).start()
        along_x(a, 0, 0).start()
        to_core(a, 0, 0, 0).start()
    def from_z(a):
        for rz in (1, 3, 2):
            along_z(a, 4 - rz).wait_recv()
            along_y(a, rz).start()
            along_x(a, 0, rz).start()
            to_core(a, 0, 0, rz).start()

    def from_y(a):
        for rz in (0, 1, 3, 2):
            along_y(a, rz).wait_recv()
            along_x(a, 1, rz).start()
            to_core(a, 0, 1, rz).start()

    def from_x(a, ry):
        for rz in (0, 1, 3, 2):
            along_x(a, ry, rz).wait_recv()
            to_core(a, 1, ry, rz).start()

    lane = lax.broadcasted_iota(jnp.int32, (TILE, LANES), 1)
    mine_half = pl.ds(pl.multiple_of(d * half, half), half)

    def weight_of(side):
        at = lax.broadcasted_iota(jnp.int32, side.shape, 1)
        mine = (at < 48) & (at % 16 == e)
        return jnp.sum(jnp.where(mine, side.astype(jnp.float32), 0.0), axis=1, keepdims=True)

    def packed(i):
        return pl.ds(i * LANES, LANES)

    def forward(rx):
        first = lax.broadcasted_iota(jnp.int32, (TILE, TILE), 0)
        second = lax.broadcasted_iota(jnp.int32, (TILE, TILE), 1)
        upto = ((second <= first) & (second // 64 == first // 64)).astype(jnp.float32).astype(jnp.bfloat16)
        base = (lax.broadcasted_iota(jnp.int32, (TILE, LANES), 0) // 64) * (LANES // 4)
        slot = (lane - base + 1).astype(jnp.float32)
        for i in range(4):
            for rz in range(4 * (i % 2)):
                to_core(0, rx, i // 2, rz).wait_recv()
            tile = 4 * rx + i
            weight = jnp.broadcast_to(weight_of(xs[tile, :, width:width + LANES]), (TILE, LANES))
            chosen = jnp.where(weight > 0.0, 1.0, 0.0)
            rank = dot_nn(upto, chosen.astype(jnp.bfloat16))
            table = jnp.where(rank == slot, chosen, 0.0).astype(jnp.bfloat16)
            place[tile] = table
            rows[packed(i), :] = dot_nn(table.T, xs[tile]).astype(jnp.bfloat16)
        weight = weight_of(rows[:, width:width + LANES])
        xhalf[rx] = rows[:, mine_half]
        for h in range(hid.shape[2] // TILE):
            cols = pl.ds(h * TILE, TILE)
            gate = dot_nn(rows[:, 0:width], wg[:, cols])
            upper = dot_nn(rows[:, 0:width], wu[:, cols])
            sigma = jax.nn.sigmoid(gate)
            silu = gate * sigma * weight
            hid[rx, :, cols] = (silu * upper).astype(jnp.bfloat16)
            dg[rx, :, cols] = (weight * upper * sigma * (1.0 + gate * (1.0 - sigma))).astype(jnp.bfloat16)
            du[rx, :, cols] = silu.astype(jnp.bfloat16)
        if rx == 0:
            spread(0, lambda cols: dot_nn(hid[0], wd[:, cols]))

    def spread(a, product):
        for n in range(width // 512):
            cols = pl.ds(n * 512, 512)
            out = product(cols).astype(jnp.bfloat16)
            for i in range(4):
                part[a, i, :, cols] = dot_nn(place[i], out[i * LANES:(i + 1) * LANES]).astype(jnp.bfloat16)
        for ry in (0, 1):
            sum_core(a, ry).start()

    def backward(rx):
        for i in range(4):
            for rz in range(4 * (i % 2)):
                to_core(1, rx, i // 2, rz).wait_recv()
            tile = 4 * rx + i
            table = place[tile].astype(jnp.float32)
            blank = jnp.zeros((TAIL, LANES), jnp.float32)
            heads = [table[64 * rz:64 * rz + 48] for rz in range(4)]
            tails = [t for rz in range(4) for t in (blank, table[64 * rz + 48:64 * rz + 56])]
            table = jnp.concatenate(heads + tails, axis=0).astype(jnp.bfloat16)
            grads = jnp.concatenate(
                [gs[tile]] + [xs[tile, 64 * rz + 48:64 * rz + 64, 0:width] for rz in range(4)], axis=0)
            rows[packed(i), 0:width] = dot_nn(table.T, grads).astype(jnp.bfloat16)
        ghalf[rx] = rows[:, mine_half]
        for h in range(hid.shape[2] // TILE):
            cols = pl.ds(h * TILE, TILE)
            d_hidden = dot_nt(rows[:, 0:width], wd[cols, :])
            dg[rx, :, cols] = (d_hidden * dg[rx, :, cols].astype(jnp.float32)).astype(jnp.bfloat16)
            du[rx, :, cols] = (d_hidden * du[rx, :, cols].astype(jnp.float32)).astype(jnp.bfloat16)
        if rx == 0:
            spread(1, lambda cols: dot_nt(dg[0], wg[cols, :]) + dot_nt(du[0], wu[cols, :]))

    def rcopy(src, dst, a, sem, device):
        return pltpu.make_async_remote_copy(
            src_ref=src, dst_ref=dst, send_sem=rsend.at[a, sem], recv_sem=rrecv.at[a, sem],
            device_id=device, device_id_type=pl.DeviceIdType.MESH)

    def sum_core(a, ry):
        return rcopy(part.at[a, 2 * ry + 1], s1.at[a, ry], a, ry, sibling)

    def sum_y(a):
        return rcopy(part.at[a, 2], s2.at[a], a, 2, across_y)

    def sum_z(a, rz):
        return rcopy(part.at[a, 0, pl.ds(rz * ROWS[0], ROWS[0])], s3.at[a, 3 - rz], a, 2 + rz, peer(0, 0, rz, 0))

    def add(a, tile, other):
        total = part[a, tile].astype(jnp.float32) + other.astype(jnp.float32)
        part[a, tile] = total.astype(jnp.bfloat16)

    def sums_over_core(a):
        sum_core(a, 1).wait_recv()
        add(a, 2, s1[a, 1])
        sum_y(a).start()
        sum_core(a, 0).wait_recv()
        add(a, 0, s1[a, 0])

    def sums_over_y(a):
        sum_y(a).wait_recv()
        add(a, 0, s2[a])
        for rz in (1, 2, 3):
            sum_z(a, rz).start()

    from_z(0)
    from_y(0)
    for load in loads:
        load.wait()
    forward(0)
    from_z(1)
    from_x(0, 0)
    sums_over_core(0)
    from_y(1)
    backward(0)
    from_x(0, 1)
    sums_over_core(1)
    sums_over_y(0)
    forward(1)
    from_x(1, 0)
    sums_over_y(1)

    def weight_grads(rx):
        def store(out, block, product):
            if rx == 1:
                product = product + out[block, :].astype(jnp.float32)
            out[block, :] = product.astype(jnp.bfloat16)

        def grads_in(j, carry):
            block = pl.ds(pl.multiple_of(j * 512, 512), 512)
            xt = xhalf[rx, :, block].T
            store(gg_out, block, dot_nn(xt, dg[rx]))
            store(gu_out, block, dot_nn(xt, du[rx]))
            return carry

        def grads_down(j, carry):
            block = pl.ds(pl.multiple_of(j * 384, 384), 384)
            store(gd_out, block, dot_nn(hid[rx, :, block].T, ghalf[rx]))
            return carry

        lax.fori_loop(0, half // 512, grads_in, 0)
        lax.fori_loop(0, hid.shape[2] // 384, grads_down, 0)

    weight_grads(0)
    from_x(1, 1)
    backward(1)
    weight_grads(1)

    for a, out in ((0, mixed_out), (1, gt_out)):
        total = part[a, 0, 0:ROWS[0]].astype(jnp.float32)
        for rz in (1, 2, 3):
            sum_z(a, rz).wait_recv()
        for i in range(3):
            total = total + s3[a, i].astype(jnp.float32)
        out[...] = total[0:tok].astype(jnp.bfloat16)

    for a in (0, 1):
        for rz in (1, 2, 3):
            along_z(a, rz).wait_send()
            sum_z(a, rz).wait_send()
        for rz in range(4):
            along_y(a, rz).wait_send()
            for r in (0, 1):
                along_x(a, r, rz).wait_send()
                for rx in (0, 1):
                    to_core(a, rx, r, rz).wait_send()
        for r in (0, 1):
            sum_core(a, r).wait_send()
        sum_y(a).wait_send()


def fused_device(tokens, expert_ids, combine, w_gate, w_up, w_down, grad_out):
    tok, width = tokens.shape
    hidden = w_gate.shape[2]
    table = weight_table(expert_ids, combine, lax.axis_size("expert"))
    high = lax.reduce_precision(table, 8, 7)
    mid = lax.reduce_precision(table - high, 8, 7)
    side = jnp.concatenate([high, mid, table - high - mid], axis=1).astype(jnp.bfloat16)
    side = jnp.pad(side, ((0, ROWS[0] - tok), (0, LANES - side.shape[1])))
    bf16 = jnp.bfloat16
    vmem = pl.BlockSpec(memory_space=pltpu.VMEM)
    hbm = pl.BlockSpec(memory_space=pl.ANY)
    mixed, grad_tokens, grad_g, grad_u, grad_d = pl.pallas_call(
        fused_kernel,
        out_shape=[
            jax.ShapeDtypeStruct((tok, width), bf16),
            jax.ShapeDtypeStruct((tok, width), bf16),
            jax.ShapeDtypeStruct((width // 2, hidden), bf16),
            jax.ShapeDtypeStruct((width // 2, hidden), bf16),
            jax.ShapeDtypeStruct((hidden, width // 2), bf16),
        ],
        in_specs=[vmem, vmem, vmem, hbm, hbm, hbm],
        out_specs=[vmem] * 5,
        scratch_shapes=[
            pltpu.VMEM((8, TILE, width + LANES), bf16),
            pltpu.VMEM((8, 4 * ROWS[1], width), bf16),
            pltpu.VMEM((width, hidden), bf16),
            pltpu.VMEM((width, hidden), bf16),
            pltpu.VMEM((hidden, width), bf16),
            pltpu.VMEM((2, 2 * TILE, hidden), bf16),
            pltpu.VMEM((2, 2 * TILE, hidden), bf16),
            pltpu.VMEM((2, 2 * TILE, hidden), bf16),
            pltpu.VMEM((2, 2 * TILE, width // 2), bf16),
            pltpu.VMEM((2, 2 * TILE, width // 2), bf16),
            pltpu.VMEM((8, TILE, LANES), bf16),
            pltpu.VMEM((2 * TILE, width + LANES), bf16),
            pltpu.VMEM((2, 4, TILE, width), bf16),
            pltpu.VMEM((2, 2, TILE, width), bf16),
            pltpu.VMEM((2, TILE, width), bf16),
            pltpu.VMEM((2, 3, ROWS[0], width), bf16),
            pltpu.SemaphoreType.DMA((3,)),
            pltpu.SemaphoreType.DMA((2, 31)),
            pltpu.SemaphoreType.DMA((2, 31)),
            pltpu.SemaphoreType.DMA((2, 6)),
            pltpu.SemaphoreType.DMA((2, 6)),
        ],
        compiler_params=pltpu.CompilerParams(
            collective_id=0, has_side_effects=True, vmem_limit_bytes=63 * 1024 * 1024),
    )(tokens, side, grad_out, w_gate[0], w_up[0], w_down[0])
    return mixed, grad_tokens, grad_g[None], grad_u[None], grad_d[None]


def solution(mesh):
    rows = P(("dp", "expert"), None)
    expert = P("expert", None, None)
    small = mesh.shape["dp"] == 2 and mesh.shape["expert"] == 16
    return jax.shard_map(
        fused_device if small else on_device,
        mesh=mesh,
        in_specs=(rows, rows, rows, expert, expert, expert, rows),
        out_specs=(rows, rows, P("expert", "dp", None), P("expert", "dp", None), P("expert", None, "dp")),
        check_vma=False,
    )
```
